32 devices in a mesh: replica: 4 (over z), fsdp: 8 (over y, x, core).
Axes of the slice: x: 2, y: 2, z: 4, core: 2. Of those that a mesh axis runs over, the one named last changes fastest.
Arguments:
- hidden_states: bfloat16 [32768, 4096], P(('replica', 'fsdp')), may hold values from -6 to 6
- cotangent: bfloat16 [32768, 1024], P(('replica', 'fsdp')), may hold values from -0.0625 to 0.0625
- key_weight: bfloat16 [4, 4096, 1024], P('replica', 'fsdp'), may hold values from -0.09375 to 0.09375
- local_fragments: bfloat16 [4, 2, 4, 4096, 1024], P('replica', None, None, 'fsdp'), may hold values from -6 to 6
- global_fragments: float32 [2, 4, 4096, 1024], P(None, None, 'fsdp', 'replica'), may hold values from -6 to 6
- momentum: float32 [2, 4, 4096, 1024], P(None, None, 'fsdp', 'replica'), may hold values from -3 to 3
- fragment_index: int32 [1], replicated, may hold values from 0 to 4095
Outputs:
- projected: bfloat16 [32768, 1024], P(('replica', 'fsdp'))
- weight_grad: float32 [4, 4096, 1024], P('replica', 'fsdp')
- new_global: float32 [2, 4, 4096, 1024], P(None, None, 'fsdp', 'replica')
- new_momentum: float32 [2, 4, 4096, 1024], P(None, None, 'fsdp', 'replica')
- synced: bfloat16 [4, 4096, 1024], P(None, 'fsdp')
The draws below stay inside these ranges and needn't reach their ends.
All inputs are finite; a program needn't handle non-finite values.
Results may differ from the reference program's by a relative error of at most 0.0095.
Values may be sent and summed in bfloat16 or wider, within the bound.
No kernel may reach another device: no remote copies, remote signals or barrier semaphores. Data moves between devices by JAX's collectives and lax.ppermute only.
A program may use at most 192 MiB of HBM per device.

```python
import jax
import jax.numpy as jnp
from jax import lax

D = 4096
KV = 1024
TOK_DEV = 1024
FRAGS = 2
FLAYERS = 4
TOKENS = 32768
N_REPLICA = 4
N_FSDP = 8


def block_levels(own_key, dims, pieces, least, largest):
    factor_of = 1.0
    for dim, shards_of in pieces:
        steps = jax.random.uniform(jax.random.fold_in(jax.random.fold_in(own_key, 6), dim), (shards_of,), jnp.float32, least / len(pieces), largest / len(pieces))
        factor_of = factor_of * jnp.repeat(jnp.exp(steps), dims[dim] // shards_of).reshape((-1,) + (1,) * (len(dims) - 1 - dim))
    return factor_of


def gaussian(rng, dims, scale, reach, split=(), held_as=jnp.bfloat16):
    factor_of = block_levels(rng, dims, split, -0.22, 0.18) if split else 1.0
    drawn = jax.random.normal(rng, dims, jnp.float32) * scale * factor_of
    return jnp.minimum(jnp.maximum(drawn, -reach), reach).astype(held_as)


def setup_inputs(seed: int = 0) -> dict:
    streams_of = jax.random.split(jax.random.key(seed), 8)
    return {
        "hidden_states": gaussian(streams_of[0], (TOKENS, D), 1.0, 6.0, ((0, 32),)),
        "cotangent": gaussian(streams_of[1], (TOKENS, KV), (1.0 / (TOK_DEV * N_FSDP) ** 0.5), 0.0625, ((0, 32),)),
        "key_weight": gaussian(streams_of[2], (N_REPLICA, D, KV), D ** -0.5, 0.09375, ((0, 4), (1, 8))),
        "local_fragments": gaussian(streams_of[3], (N_REPLICA, FRAGS, FLAYERS, D, KV), 1.0, 6.0, ((0, 4), (3, 8))),
        "global_fragments": gaussian(streams_of[4], (FRAGS, FLAYERS, D, KV), 1.0, 6.0, ((2, 8), (3, 4)), jnp.float32),
        "momentum": gaussian(streams_of[5], (FRAGS, FLAYERS, D, KV), 0.5, 3.0, ((2, 8), (3, 4)), jnp.float32),
        "fragment_index": jax.random.randint(streams_of[6], (1,), 0, 4096).astype(jnp.int32),
    }


def reference(hidden_states, cotangent, key_weight, local_fragments, global_fragments, momentum, fragment_index):
    group_tokens = TOK_DEV * N_FSDP
    states = hidden_states.reshape(N_REPLICA, group_tokens, D)
    cotans = cotangent.reshape(N_REPLICA, group_tokens, KV)

    def per_replica(items):
        block_states, block_cotan, weights = items
        keys = jnp.dot(block_states, weights, preferred_element_type=jnp.float32).astype(jnp.bfloat16)
        gradient = jnp.dot(block_states.T, block_cotan, preferred_element_type=jnp.float32)
        return keys, gradient

    projected, weight_grad = lax.map(per_replica, (states, cotans, key_weight))
    projected = projected.reshape(TOKENS, KV)
    chosen = fragment_index[0] % FRAGS
    locals_chosen = lax.dynamic_index_in_dim(local_fragments, chosen, 1, keepdims=False)
    mean_local = jnp.mean(locals_chosen.astype(jnp.float32), axis=0)
    global_chosen = lax.dynamic_index_in_dim(global_fragments, chosen, 0, keepdims=False)
    moment_chosen = lax.dynamic_index_in_dim(momentum, chosen, 0, keepdims=False)
    pseudo = global_chosen - mean_local
    moment_next = 0.9 * moment_chosen + pseudo
    global_next = global_chosen - 0.7 * (pseudo + 0.9 * moment_next)
    new_momentum = lax.dynamic_update_index_in_dim(momentum, moment_next, chosen, 0)
    new_global = lax.dynamic_update_index_in_dim(global_fragments, global_next, chosen, 0)
    synced = global_next.astype(jnp.bfloat16)
    return projected, weight_grad, new_global, new_momentum, synced
```

```python
import functools

import jax
import jax.numpy as jnp
from jax import lax
from jax.experimental import pallas as pl
from jax.experimental.pallas import tpu as pltpu
from jax.sharding import PartitionSpec as P

FRAGS = 2
PIECES = 10
STEPS = 1
DELAY = 2
PROJECT_BLOCKS = 4
MEAN_PART = 1.33
GLOBAL_PART = -0.33
MOMENT_PART = -0.567
F32 = jnp.float32
BF16 = jnp.bfloat16
ANY = pl.BlockSpec(memory_space=pl.ANY)
CONTRACT_ROWS = (((0,), (0,)), ((), ()))
CHOSEN, REPLICA, FSDP = 0, 1, 2
VMEM = 16 << 20
LONG = 1 << 30


def in_hbm(x):
    return pltpu.with_memory_space_constraint(x, pltpu.HBM)


class Chain:
    def __init__(self, scalars):
        self.scalars, self.token = scalars, None


def call(body, name, chain, operands, in_specs, out_shape, out_specs, grid, aliases=None, copies=(), cost=0):
    n_in, n_out, n = len(operands), len(out_shape), len(copies)
    aliases = dict(aliases or {})
    operands, in_specs = list(operands), list(in_specs)
    out_shape, out_specs = list(out_shape), list(out_specs)
    unread = []
    for k, (array, in_spec, space, shape, out_spec, into) in enumerate(copies):
        operands.append(array)
        in_specs.append(in_spec)
        out_shape.append(space(shape, array.dtype))
        out_specs.append(out_spec)
        if into is not None:
            aliases[1 + n_in + n + len(unread)] = n_out + k
            unread.append(into)
    if chain.token is not None:
        unread.append(chain.token)
    operands += unread
    out_shape.append(jax.ShapeDtypeStruct((8, 128), F32))

    def kernel(s, *refs):
        outs = refs[len(operands) :]
        body(s, *refs[:n_in], *outs[:n_out])
        for source, target in zip(refs[n_in : n_in + n], outs[n_out:]):
            target[...] = source[...].reshape(target.shape)

    *results, chain.token = pl.pallas_call(
        kernel,
        out_shape=out_shape,
        grid_spec=pltpu.PrefetchScalarGridSpec(
            num_scalar_prefetch=1,
            grid=grid,
            in_specs=in_specs + [ANY] * len(unread),
            out_specs=out_specs + [ANY],
        ),
        input_output_aliases=aliases,
        compiler_params=pltpu.CompilerParams(vmem_limit_bytes=VMEM),
        cost_estimate=pl.CostEstimate(flops=0, bytes_accessed=cost, transcendentals=0),
        name=name,
    )(chain.scalars, *operands)
    return results


class Fsdp:
    def __init__(self, hidden_states, cotangent, weight, chain):
        self.states, self.cotans = in_hbm(hidden_states), in_hbm(cotangent)
        self.tokens, self.model = hidden_states.shape
        self.keys = cotangent.shape[1]
        self.devices = lax.axis_size("fsdp")
        self.rows = self.model // self.devices
        self.chain = chain
        self.whole = pl.BlockSpec((self.tokens, self.keys), lambda i, s: (0, 0))
        self.weight = in_hbm(lax.all_gather(weight, "fsdp", axis=0, tiled=True))
        self.sums = None

    def project(self, part):
        block, depth = self.tokens // PROJECT_BLOCKS, self.model // 4
        first, final = part == 0, part == 3
        rows = pl.BlockSpec((block, self.keys), lambda i, s: (i, 0))
        operands = [self.states, self.weight]
        in_specs = [
            pl.BlockSpec((block, depth), lambda i, s: (i, part)),
            pl.BlockSpec((depth, self.keys), lambda i, s: (part, 0)),
        ]
        aliases = {}
        if not first:
            operands.append(self.total)
            in_specs.append(rows)
            aliases = {} if final else {3: 0}

        def body(s, states, weight, *refs):
            total = jnp.dot(states[...], weight[...], preferred_element_type=F32)
            if not first:
                total = total + refs[0][...]
            refs[-1][...] = total.astype(refs[-1].dtype)

        (self.total,) = call(
            body, f"project_{part}", self.chain, operands, in_specs,
            [pltpu.HBM((self.tokens, self.keys), BF16) if final else pltpu.VMEM((self.tokens, self.keys), F32)], [rows],
            (PROJECT_BLOCKS,), aliases,
        )

    def grad(self, first, n, copies=()):
        def body(s, states, cotans, *refs):
            refs[-1][0] = lax.dot_general(
                states[...], cotans[...], CONTRACT_ROWS, preferred_element_type=F32
            ).astype(BF16)

        operands = [self.states, self.cotans]
        in_specs = [pl.BlockSpec((self.tokens, self.rows), lambda i, s: (0, first + i)), self.whole]
        aliases = {}
        if self.sums is not None:
            operands.append(self.sums)
            in_specs.append(ANY)
            aliases = {3: 0}
        self.sums, *copied = call(
            body, f"grad_{first}", self.chain, operands, in_specs,
            [pltpu.HBM((self.devices, self.rows, self.keys), BF16)],
            [pl.BlockSpec((1, self.rows, self.keys), lambda i, s: (first + i, 0, 0))],
            (n,), aliases, copies=copies,
        )
        return copied

    def scatter(self):
        self.sums = lax.psum_scatter(
            self.sums.reshape(self.model, self.keys), "fsdp", scatter_dimension=0, tiled=True
        )

    def widen(self):
        def body(s, x, out):
            out[...] = x[...].astype(F32)

        each = pl.BlockSpec((self.rows // 2, self.keys), lambda i, s: (i, 0))
        (out,) = call(
            body, "widen", self.chain, [self.sums], [each], [pltpu.HBM((self.rows, self.keys), F32)], [each], (2,)
        )
        return out


def own_term(g, m, replicas):
    return (GLOBAL_PART * g + MOMENT_PART * m) * (replicas / MEAN_PART)


def by_replica(replicas, s, body):
    for z in range(replicas):
        pl.when(s[REPLICA] == z)(functools.partial(body, z))


def way(z, side):
    return (z - 1 + side) % 2


def hops_of(z, replicas):
    return z - 1, replicas - 2 - z


def first_body(replicas, s, l, g, m, out):
    width = g.shape[2]

    def body(z):
        if 0 < z < replicas - 1:
            return
        columns = slice(z * width, (z + 1) * width)
        out[...] = l[0]
        out[:, columns] = (l[0, :, columns].astype(F32) + own_term(g[0], m[0], replicas)).astype(BF16)

    by_replica(replicas, s, body)


def round_body(replicas, old_of, ways, outs, keep, s, *refs):
    refs = list(refs)
    take = lambda n: [refs.pop(0) for _ in range(n)]
    came = take(2)
    old = dict(zip(old_of, take(len(old_of))))
    sources = take(3), take(3)
    width = sources[0][1].shape[2]
    kept = take(3) if outs else ()
    targets = take(ways)
    results = take(3) if outs else ()

    def body(z):
        columns = slice(z * width, (z + 1) * width)
        hops = hops_of(z, replicas)
        for side in (0, 1):
            target = way(z, 1 - side)
            if hops[1 - side] < 0 or target >= ways:
                continue
            l, g, m = sources[side]
            out = targets[target]
            if hops[side] < 0:
                out[...] = l[0]
                mine = l[0, :, columns].astype(F32)
            else:
                total = came[way(z, side)][...].astype(F32) + l[0].astype(F32)
                out[...] = total.astype(BF16)
                mine = total[:, columns]
            out[:, columns] = (mine + own_term(g[0], m[0], replicas)).astype(BF16)
        if not outs:
            return
        reach = max(hops)
        if reach in keep:
            for ref, before in zip(results, kept):
                ref[...] = before[...]
            return
        l, g, m = sources[0 if hops[0] == reach else 1]
        total = l[0].astype(F32)
        for side in (0, 1):
            if hops[side] >= 0:
                path = way(z, side)
                total = total + old.get((path, reach - hops[side]), came[path])[...].astype(F32)
        synced, new_g, new_m = results
        synced[...] = (total * (MEAN_PART / replicas)).astype(BF16)
        mean = total[:, columns] / replicas
        pseudo = g[0] - mean
        moment = 0.9 * m[0] + pseudo
        after = g[0] - 0.7 * (pseudo + 0.9 * moment)
        synced[:, columns] = after.astype(BF16)
        new_g[0] = after
        new_m[0] = moment

    by_replica(replicas, s, body)


class Line:
    def __init__(self, local_fragments, global_fragments, momentum, chain):
        self.replicas = lax.axis_size("replica")
        frags, layers, rows, keys = local_fragments.shape
        self.given = global_fragments.shape
        self.layers, self.rows, self.keys = layers, rows, keys
        self.width = global_fragments.shape[3]
        self.total = layers * rows
        unit = 16 * STEPS
        self.chunk = -(-self.total // (unit * PIECES)) * unit
        self.block = self.chunk // STEPS
        self.pieces = -(-self.total // self.chunk)
        self.local = in_hbm(local_fragments.reshape(frags, self.total, keys))
        self.outer = in_hbm(global_fragments.reshape(frags, self.total, self.width))
        self.moment = in_hbm(momentum.reshape(frags, self.total, self.width))
        self.last = self.pieces - 1 + DELAY * (self.replicas - 2)
        self.chain = chain
        self.sources, self.staged = [self.local, self.outer, self.moment], False
        self.staged_sources, self.idled = [None] * 3, set()
        self.piece = pl.BlockSpec((self.block, keys), lambda i, s: (i, 0))
        self.piece_shape = pltpu.VMEM((self.chunk, keys), BF16)
        self.state = None
        self.ready, self.came = [], []

    def pairs(self, t, path):
        n = self.replicas
        return [
            pair
            for z in range(n - 1)
            if z % 2 == path
            for pair, hop in (((z, z + 1), z), ((z + 1, z), n - 2 - z))
            if 0 <= t - DELAY * hop < self.pieces
        ]

    def ways(self, t):
        if t > self.last:
            return 0
        return 2 if self.pairs(t, 1) else 1

    def row(self, place, i):
        start = jnp.minimum(jnp.clip(place, 0, self.pieces - 1) * self.chunk, self.total - self.chunk)
        return pl.multiple_of(start + i * self.block, 16)

    def at(self, width, place, frag=lambda s: s[CHOSEN]):
        size = (pl.Element(1), pl.Element(self.block), pl.Element(width))
        return pl.BlockSpec(size, lambda i, s: (frag(s), self.row(place(s[REPLICA]), i), 0))

    def first(self, t):
        specs = [self.at(n, lambda z: t) for n in (self.keys, self.width, self.width)]
        self.ready.append(
            call(
                functools.partial(first_body, self.replicas), "first_sends", self.chain,
                [self.local, self.outer, self.moment], specs, [self.piece_shape], [self.piece], (STEPS,),
            )
        )

    def stage(self, k, steps):
        array = self.sources[k]
        size = (1, array.shape[1] // steps, array.shape[2])
        source = pl.BlockSpec(size, lambda i, s: (s[CHOSEN], i, 0))
        target = pl.BlockSpec(size, lambda i, s: (0, i, 0))
        return array, source, pltpu.VMEM, (1,) + array.shape[1:], target, None

    def finish_idle(self, k, copied):
        if copied:
            self.state[k] = copied[0]
            self.idled.add(k)

    def idle(self, k, steps):
        array, state = (self.outer, self.moment)[k - 1], self.state[k]
        spec = pl.BlockSpec((1, array.shape[1] // steps, array.shape[2]), lambda i, s: (1 - s[CHOSEN], i, 0))
        return array, spec, pltpu.HBM, array.shape, spec, state

    def send(self, t):
        came = [lax.ppermute(x, "replica", self.pairs(t, path)) for path, x in enumerate(self.ready[t])]
        self.came.append((came + came)[:2])

    def round(self, t):
        n = self.replicas
        outs = t >= DELAY * min(max(hops_of(z, n)) for z in range(n))
        keep = {r for r in (max(hops_of(z, n)) for z in range(n)) if t > self.pieces - 1 + DELAY * r}
        users = {}
        for z in range(n):
            hops = hops_of(z, n)
            for side in (0, 1):
                behind = max(hops) - hops[side]
                if outs and hops[side] >= 0 and behind and t >= DELAY * behind:
                    users.setdefault((way(z, side), behind), []).append(z)
        old = [self.came[t - DELAY * behind][path] for path, behind in users]
        old_specs = [
            pl.BlockSpec(
                (self.block, self.keys),
                lambda i, s, zs=zs: (i * sum((s[REPLICA] == z).astype(jnp.int32) for z in zs), 0),
            )
            for zs in users.values()
        ]
        to_right = lambda z: t + DELAY - DELAY * z
        to_left = lambda z: t + DELAY - DELAY * (n - 1 - z)
        frag = (lambda s: 0) if self.staged else (lambda s: s[CHOSEN])
        specs = [self.at(w, place, frag) for place in (to_right, to_left) for w in (self.keys, self.width, self.width)]
        in_specs = [self.piece, self.piece] + old_specs + specs
        operands = list(self.came[t]) + old + self.sources * 2
        ways = self.ways(t + DELAY)
        out_shape, out_specs, aliases = [self.piece_shape] * ways, [self.piece] * ways, {}
        if outs:
            place = lambda z: t - DELAY * jnp.maximum(z - 1, n - 2 - z)
            flat = pl.BlockSpec(
                (pl.Element(self.block), pl.Element(self.keys)), lambda i, s: (self.row(place(s[REPLICA]), i), 0)
            )
            state_specs = [flat] + [self.at(self.width, place)] * 2
            if self.state is None:
                operands += [self.came[t][0]] * 3
                in_specs += [ANY] * 3
            else:
                aliases = {1 + len(operands) + k: ways + k for k in range(3)}
                operands += self.state
                in_specs += state_specs if keep else [ANY] * 3
            out_shape += [
                pltpu.HBM((self.total, self.keys), BF16),
                pltpu.HBM(self.outer.shape, F32),
                pltpu.HBM(self.moment.shape, F32),
            ]
            out_specs += state_specs
        if not out_shape:
            return
        results = call(
            functools.partial(round_body, n, list(users), ways, outs, keep), f"round_{t}", self.chain, operands, in_specs,
            out_shape, out_specs, (STEPS,), aliases, cost=LONG if t == self.last else 0,
        )
        self.ready.append(results[:ways])
        if outs:
            self.state = list(results[ways:])

    def result(self):
        for k in (1, 2):
            if k not in self.idled:
                copies = [self.idle(k, 4)]
                self.finish_idle(k, call(lambda s: None, "idle", self.chain, [], [], [], [], (4,), copies=copies))
        synced, new_global, new_momentum = self.state
        return (
            synced.reshape(self.layers, self.rows, self.keys),
            new_global.reshape(self.given),
            new_momentum.reshape(self.given),
        )


def shards(
    hidden_states,
    cotangent,
    key_weight,
    local_fragments,
    global_fragments,
    momentum,
    fragment_index,
):
    chosen = fragment_index[0] % FRAGS
    place = [lax.axis_index("replica"), lax.axis_index("fsdp")]
    chain = Chain(jnp.stack([chosen] + place).astype(jnp.int32))
    line = Line(local_fragments[0], global_fragments, momentum, chain)
    fsdp = Fsdp(hidden_states, cotangent, key_weight[0], chain)
    eighth = fsdp.devices // 8

    def grad(first, n, stage=(), idle=None):
        steps = n * eighth
        copies = [line.stage(k, steps) for k in stage]
        if idle and line.state:
            copies = [line.idle(idle, steps)]
        copied = fsdp.grad(first * eighth, steps, copies)
        for k, array in zip(stage, copied):
            line.staged_sources[k] = array
        if idle:
            line.finish_idle(idle, copied)

    def work(t):
        if t == 0:
            grad(0, 2, stage=(0,))
        elif t == 1:
            grad(2, 2, stage=(1, 2))
            line.sources, line.staged = line.staged_sources, True
        elif t == 2:
            grad(4, 2, idle=1)
        elif t == 3:
            grad(6, 2, idle=2)
            fsdp.scatter()
        elif 6 <= t < 10:
            fsdp.project(t - 6)

    for t in range(DELAY):
        line.first(t)
    for t in range(line.last + 1):
        line.send(t)
        line.round(t)
        work(t)
    synced, new_global, new_momentum = line.result()
    weight_grad = fsdp.widen()
    return (fsdp.total, weight_grad[None], new_global, new_momentum, synced)


def solution(mesh):
    placed = (
        P(("replica", "fsdp"), None),
        P(("replica", "fsdp"), None),
        P("replica", "fsdp", None),
        P("replica", None, None, "fsdp", None),
        P(None, None, "fsdp", "replica"),
        P(None, None, "fsdp", "replica"),
        P(),
    )
    return jax.shard_map(
        shards,
        mesh=mesh,
        in_specs=placed,
        out_specs=(
            P(("replica", "fsdp"), None),
            P("replica", "fsdp", None),
            P(None, None, "fsdp", "replica"),
            P(None, None, "fsdp", "replica"),
            P(None, "fsdp", None),
        ),
        check_vma=False,
    )
```

```python
import functools

import jax
import jax.numpy as jnp
from jax import lax
from jax.experimental import pallas as pl
from jax.experimental.pallas import tpu as pltpu
from jax.sharding import PartitionSpec as P

FRAGS = 2
PIECES = 8
STEPS = 1
DELAY = 2
PROJECT_BLOCKS = 4
GRADS = ((0, 2, (0,), -1), (2, 3, (1, 2), 0), (5, 3, (), 2))
IDLE_BEFORE = 1
PROJECT_ROUNDS = (5, 8)
MEAN_PART = 1.33
GLOBAL_PART = -0.33
MOMENT_PART = -0.567
F32 = jnp.float32
BF16 = jnp.bfloat16
ANY = pl.BlockSpec(memory_space=pl.ANY)
CONTRACT_ROWS = (((0,), (0,)), ((), ()))
CHOSEN, REPLICA, FSDP = 0, 1, 2
VMEM = 18 << 20
VMEM_R = 10 << 20
VMEM_P = 16 << 20
LONG = 112 * 10**9


def in_vmem(x):
    return pltpu.with_memory_space_constraint(x, pltpu.VMEM)


def in_hbm(x):
    return pltpu.with_memory_space_constraint(x, pltpu.HBM)


class Chain:
    def __init__(self, scalars):
        self.scalars, self.token = scalars, None


def call(body, name, chain, operands, in_specs, out_shape, out_specs, grid, aliases=None, copies=(), cost=0, vmem=VMEM):
    n_in, n_out, n = len(operands), len(out_shape), len(copies)
    aliases = dict(aliases or {})
    operands, in_specs = list(operands), list(in_specs)
    out_shape, out_specs = list(out_shape), list(out_specs)
    unread = []
    for k, (array, in_spec, space, shape, out_spec, into) in enumerate(copies):
        operands.append(array)
        in_specs.append(in_spec)
        out_shape.append(space(shape, array.dtype))
        out_specs.append(out_spec)
        if into is not None:
            aliases[1 + n_in + n + len(unread)] = n_out + k
            unread.append(into)
    if chain.token is not None:
        unread.append(chain.token)
    operands += unread
    out_shape.append(jax.ShapeDtypeStruct((8, 128), F32))

    def kernel(s, *refs):
        outs = refs[len(operands) :]
        body(s, *refs[:n_in], *outs[:n_out])
        for source, target in zip(refs[n_in : n_in + n], outs[n_out:]):
            target[...] = source[...].reshape(target.shape)

    *results, chain.token = pl.pallas_call(
        kernel,
        out_shape=out_shape,
        grid_spec=pltpu.PrefetchScalarGridSpec(
            num_scalar_prefetch=1,
            grid=grid,
            in_specs=in_specs + [ANY] * len(unread),
            out_specs=out_specs + [ANY],
        ),
        input_output_aliases=aliases,
        compiler_params=pltpu.CompilerParams(vmem_limit_bytes=vmem),
        cost_estimate=pl.CostEstimate(flops=cost, bytes_accessed=0, transcendentals=0),
        name=name,
    )(chain.scalars, *operands)
    return results


class Fsdp:
    def __init__(self, hidden_states, cotangent, weight, chain):
        self.states, self.cotans = in_hbm(hidden_states), in_hbm(cotangent)
        self.tokens, self.model = hidden_states.shape
        self.keys = cotangent.shape[1]
        self.devices = lax.axis_size("fsdp")
        self.rows = self.model // self.devices
        self.chain = chain
        self.whole = pl.BlockSpec((self.tokens, self.keys), lambda i, s: (0, 0), pipeline_mode=pl.Buffered(1))
        self.weight = in_hbm(lax.all_gather(weight, "fsdp", axis=0, tiled=True))
        self.sums = None

    def project(self, part, parts):
        block, depth = self.tokens // PROJECT_BLOCKS, self.model // parts
        first, final = part == 0, part == parts - 1
        rows = pl.BlockSpec((block, self.keys), lambda i, s: (i, 0))
        operands = [self.states, self.weight]
        in_specs = [
            pl.BlockSpec((block, depth), lambda i, s: (i, part)),
            pl.BlockSpec((depth, self.keys), lambda i, s: (part, 0), pipeline_mode=pl.Buffered(1)),
        ]
        aliases = {}
        if not first:
            operands.append(self.total)
            in_specs.append(rows)
            aliases = {} if final else {3: 0}

        def body(s, states, weight, *refs):
            total = jnp.dot(states[...], weight[...], preferred_element_type=F32)
            if not first:
                total = total + refs[0][...]
            refs[-1][...] = total.astype(refs[-1].dtype)

        (self.total,) = call(
            body, f"project_{part}", self.chain, operands, in_specs,
            [pltpu.HBM((self.tokens, self.keys), BF16) if final else pltpu.VMEM((self.tokens, self.keys), F32)], [rows],
            (PROJECT_BLOCKS,), aliases, vmem=VMEM_P,
        )

    def grad(self, first, n, copies=()):
        def body(s, states, cotans, *refs):
            refs[-1][0] = lax.dot_general(
                states[...], cotans[...], CONTRACT_ROWS, preferred_element_type=F32
            ).astype(BF16)

        operands = [self.states, self.cotans]
        in_specs = [pl.BlockSpec((self.tokens, self.rows), lambda i, s: (0, first + i)), self.whole]
        aliases = {}
        if self.sums is not None:
            operands.append(self.sums)
            in_specs.append(ANY)
            aliases = {3: 0}
        self.sums, *copied = call(
            body, f"grad_{first}", self.chain, operands, in_specs,
            [pltpu.HBM((self.devices, self.rows, self.keys), BF16)],
            [pl.BlockSpec((1, self.rows, self.keys), lambda i, s: (first + i, 0, 0))],
            (n,), aliases, copies=copies,
        )
        return copied

    def scatter(self):
        self.sums = lax.psum_scatter(
            self.sums.reshape(self.model, self.keys), "fsdp", scatter_dimension=0, tiled=True
        )

    def widen(self):
        def body(s, x, out):
            out[...] = x[...].astype(F32)

        each = pl.BlockSpec((self.rows // 2, self.keys), lambda i, s: (i, 0))
        (out,) = call(
            body, "widen", self.chain, [in_hbm(self.sums)], [each], [pltpu.HBM((self.rows, self.keys), F32)], [each], (2,)
        )
        return out


def own_term(g, m, replicas):
    return (GLOBAL_PART * g + MOMENT_PART * m) * (replicas / MEAN_PART)


def by_replica(replicas, s, body):
    for z in range(replicas):
        pl.when(s[REPLICA] == z)(functools.partial(body, z))


def way(z, side):
    return (z - 1 + side) % 2


def hops_of(z, replicas):
    return z - 1, replicas - 2 - z


def first_body(replicas, s, l, g, m, out):
    width = g.shape[2]

    def body(z):
        if 0 < z < replicas - 1:
            return
        columns = slice(z * width, (z + 1) * width)
        out[...] = l[0]
        out[:, columns] = (l[0, :, columns].astype(F32) + own_term(g[0], m[0], replicas)).astype(BF16)

    by_replica(replicas, s, body)


def round_body(replicas, old_of, ways, outs, keep, s, *refs):
    refs = list(refs)
    take = lambda n: [refs.pop(0) for _ in range(n)]
    came = take(2)
    old = dict(zip(old_of, take(len(old_of))))
    sources = take(3), take(3)
    width = sources[0][1].shape[2]
    kept = take(3) if outs else ()
    targets = take(ways)
    results = take(3) if outs else ()

    def body(z):
        columns = slice(z * width, (z + 1) * width)
        hops = hops_of(z, replicas)
        for side in (0, 1):
            target = way(z, 1 - side)
            if hops[1 - side] < 0 or target >= ways:
                continue
            l, g, m = sources[side]
            out = targets[target]
            if hops[side] < 0:
                out[...] = l[0]
                mine = l[0, :, columns].astype(F32)
            else:
                total = came[way(z, side)][...].astype(F32) + l[0].astype(F32)
                out[...] = total.astype(BF16)
                mine = total[:, columns]
            out[:, columns] = (mine + own_term(g[0], m[0], replicas)).astype(BF16)
        if not outs:
            return
        reach = max(hops)
        if reach in keep:
            for ref, before in zip(results, kept):
                ref[...] = before[...]
            return
        l, g, m = sources[0 if hops[0] == reach else 1]
        total = l[0].astype(F32)
        for side in (0, 1):
            if hops[side] >= 0:
                path = way(z, side)
                total = total + old.get((path, reach - hops[side]), came[path])[...].astype(F32)
        synced, new_g, new_m = results
        synced[...] = (total * (MEAN_PART / replicas)).astype(BF16)
        mean = total[:, columns] / replicas
        pseudo = g[0] - mean
        moment = 0.9 * m[0] + pseudo
        after = g[0] - 0.7 * (pseudo + 0.9 * moment)
        synced[:, columns] = after.astype(BF16)
        new_g[0] = after
        new_m[0] = moment

    by_replica(replicas, s, body)


class Line:
    def __init__(self, local_fragments, global_fragments, momentum, chain):
        self.replicas = lax.axis_size("replica")
        frags, layers, rows, keys = local_fragments.shape
        self.given = global_fragments.shape
        self.layers, self.rows, self.keys = layers, rows, keys
        self.width = global_fragments.shape[3]
        self.total = layers * rows
        unit = 16 * STEPS
        self.chunk = -(-self.total // (unit * PIECES)) * unit
        self.block = self.chunk // STEPS
        self.pieces = -(-self.total // self.chunk)
        self.local = in_hbm(local_fragments.reshape(frags, self.total, keys))
        self.outer = in_hbm(global_fragments.reshape(frags, self.total, self.width))
        self.moment = in_hbm(momentum.reshape(frags, self.total, self.width))
        self.last = self.pieces - 1 + DELAY * (self.replicas - 2)
        self.chain = chain
        self.sources, self.staged = [self.local, self.outer, self.moment], False
        self.staged_sources = [None] * 3
        self.piece = pl.BlockSpec((self.block, keys), lambda i, s: (i, 0))
        self.piece_shape = pltpu.VMEM((self.chunk, keys), BF16)
        self.state = None
        self.ready, self.came = [], []

    def pairs(self, t, path):
        n = self.replicas
        return [
            pair
            for z in range(n - 1)
            if z % 2 == path
            for pair, hop in (((z, z + 1), z), ((z + 1, z), n - 2 - z))
            if 0 <= t - DELAY * hop < self.pieces
        ]

    def ways(self, t):
        if t > self.last:
            return 0
        return 2 if self.pairs(t, 1) else 1

    def row(self, place, i):
        start = jnp.minimum(jnp.clip(place, 0, self.pieces - 1) * self.chunk, self.total - self.chunk)
        return pl.multiple_of(start + i * self.block, 16)

    def at(self, width, place, frag=lambda s: s[CHOSEN]):
        size = (pl.Element(1), pl.Element(self.block), pl.Element(width))
        return pl.BlockSpec(size, lambda i, s: (frag(s), self.row(place(s[REPLICA]), i), 0))

    def first(self, t):
        specs = [self.at(n, lambda z: t) for n in (self.keys, self.width, self.width)]
        self.ready.append(
            call(
                functools.partial(first_body, self.replicas), "first_sends", self.chain,
                [self.local, self.outer, self.moment], specs, [self.piece_shape], [self.piece], (STEPS,),
            )
        )

    def stage(self, k, steps):
        array = self.sources[k]
        steps = 2 ** (steps.bit_length() - 1)
        last = steps - 1
        size = (1, array.shape[1] // steps, array.shape[2])
        source = pl.BlockSpec(size, lambda i, s: (s[CHOSEN], jnp.minimum(i, last), 0))
        target = pl.BlockSpec(size, lambda i, s: (0, jnp.minimum(i, last), 0))
        return array, source, pltpu.VMEM, (1,) + array.shape[1:], target, None

    def idle(self, k, steps):
        array, state = (self.outer, self.moment)[k - 1], self.state[k]
        spec = pl.BlockSpec((1, array.shape[1] // steps, array.shape[2]), lambda i, s: (1 - s[CHOSEN], i, 0))
        return array, spec, pltpu.HBM, array.shape, spec, state

    def idle_all(self):
        copies = [self.idle(k, 4) for k in (1, 2)]
        self.state[1:] = call(lambda s: None, "idle", self.chain, [], [], [], [], (4,), copies=copies)

    def send(self, t):
        came = [lax.ppermute(x, "replica", self.pairs(t, path)) for path, x in enumerate(self.ready[t])]
        self.came.append((came + came)[:2])

    def round(self, t):
        n = self.replicas
        outs = t >= DELAY * min(max(hops_of(z, n)) for z in range(n))
        keep = {r for r in (max(hops_of(z, n)) for z in range(n)) if t > self.pieces - 1 + DELAY * r}
        users = {}
        for z in range(n):
            hops = hops_of(z, n)
            for side in (0, 1):
                behind = max(hops) - hops[side]
                if outs and hops[side] >= 0 and behind and t >= DELAY * behind:
                    users.setdefault((way(z, side), behind), []).append(z)
        old = [self.came[t - DELAY * behind][path] for path, behind in users]
        old_specs = [
            pl.BlockSpec(
                (self.block, self.keys),
                lambda i, s, zs=zs: (i * sum((s[REPLICA] == z).astype(jnp.int32) for z in zs), 0),
            )
            for zs in users.values()
        ]
        to_right = lambda z: t + DELAY - DELAY * z
        to_left = lambda z: t + DELAY - DELAY * (n - 1 - z)
        frag = (lambda s: 0) if self.staged else (lambda s: s[CHOSEN])
        specs = [self.at(w, place, frag) for place in (to_right, to_left) for w in (self.keys, self.width, self.width)]
        in_specs = [self.piece, self.piece] + old_specs + specs
        operands = list(self.came[t]) + old + self.sources * 2
        ways = self.ways(t + DELAY)
        out_shape, out_specs, aliases = [self.piece_shape] * ways, [self.piece] * ways, {}
        if outs:
            place = lambda z: t - DELAY * jnp.maximum(z - 1, n - 2 - z)
            flat = pl.BlockSpec(
                (pl.Element(self.block), pl.Element(self.keys)), lambda i, s: (self.row(place(s[REPLICA]), i), 0)
            )
            state_specs = [flat] + [self.at(self.width, place)] * 2
            if self.state is None:
                operands += [self.came[t][0]] * 3
                in_specs += [ANY] * 3
            else:
                aliases = {1 + len(operands) + k: ways + k for k in range(3)}
                operands += self.state
                in_specs += state_specs if keep else [ANY] * 3
            out_shape += [
                pltpu.HBM((self.total, self.keys), BF16),
                pltpu.HBM(self.outer.shape, F32),
                pltpu.HBM(self.moment.shape, F32),
            ]
            out_specs += state_specs
        if not out_shape:
            return
        results = call(
            functools.partial(round_body, n, list(users), ways, outs, keep), f"round_{t}", self.chain, operands, in_specs,
            out_shape, out_specs, (STEPS,), aliases, cost=LONG if t == self.last else 0, vmem=VMEM_R,
        )
        self.ready.append(results[:ways])
        if outs:
            self.state = list(results[ways:])

    def result(self):
        synced, new_global, new_momentum = self.state
        return (
            synced.reshape(self.layers, self.rows, self.keys),
            new_global.reshape(self.given),
            new_momentum.reshape(self.given),
        )


def shards(
    hidden_states,
    cotangent,
    key_weight,
    local_fragments,
    global_fragments,
    momentum,
    fragment_index,
):
    chosen = fragment_index[0] % FRAGS
    place = [lax.axis_index("replica"), lax.axis_index("fsdp")]
    chain = Chain(jnp.stack([chosen] + place).astype(jnp.int32))
    line = Line(local_fragments[0], global_fragments, momentum, chain)
    fsdp = Fsdp(hidden_states, cotangent, key_weight[0], chain)
    eighth = fsdp.devices // 8

    def grad(first, n, stage):
        steps = n * eighth
        copied = fsdp.grad(first * eighth, steps, [line.stage(k, steps) for k in stage])
        for k, array in zip(stage, copied):
            line.staged_sources[k] = array

    def work(t):
        for first, n, stage, then in GRADS:
            if t == then:
                grad(first, n, stage)
                if None not in line.staged_sources and not line.staged:
                    line.sources, line.staged = [in_vmem(x) for x in line.staged_sources], True
                if first + n == 8:
                    fsdp.scatter()
        if t in PROJECT_ROUNDS:
            fsdp.project(PROJECT_ROUNDS.index(t), len(PROJECT_ROUNDS))
        if t == line.last - IDLE_BEFORE:
            line.idle_all()

    for t in range(DELAY):
        line.first(t)
    work(-1)
    for t in range(line.last + 1):
        line.send(t)
        line.round(t)
        work(t)
    synced, new_global, new_momentum = line.result()
    weight_grad = fsdp.widen()
    return (fsdp.total, weight_grad[None], new_global, new_momentum, synced)


def solution(mesh):
    placed = (
        P(("replica", "fsdp"), None),
        P(("replica", "fsdp"), None),
        P("replica", "fsdp", None),
        P("replica", None, None, "fsdp", None),
        P(None, None, "fsdp", "replica"),
        P(None, None, "fsdp", "replica"),
        P(),
    )
    return jax.shard_map(
        shards,
        mesh=mesh,
        in_specs=placed,
        out_specs=(
            P(("replica", "fsdp"), None),
            P("replica", "fsdp", None),
            P(None, None, "fsdp", "replica"),
            P(None, None, "fsdp", "replica"),
            P(None, "fsdp", None),
        ),
        check_vma=False,
    )
```

```python
import functools

import jax
import jax.numpy as jnp
from jax import lax
from jax.experimental import pallas as pl
from jax.experimental.pallas import tpu as pltpu
from jax.sharding import PartitionSpec as P

FRAGS = 2
PIECES = 10
STEPS = 1
DELAY = 2
PROJECT_BLOCKS = 4
GRADS = ((0, 2, (0,), -1), (2, 3, (1, 2), 0), (5, 3, (), 2))
IDLE_BEFORE = 5
PROJECT_ROUNDS = (6, 10)
MEAN_PART = 1.33
GLOBAL_PART = -0.33
MOMENT_PART = -0.567
F32 = jnp.float32
BF16 = jnp.bfloat16
ANY = pl.BlockSpec(memory_space=pl.ANY)
CONTRACT_ROWS = (((0,), (0,)), ((), ()))
CHOSEN, REPLICA, FSDP = 0, 1, 2
VMEM = 14 << 20
VMEM_R = 10 << 20
VMEM_P = 16 << 20
LONG = 116 * 10**9


def in_vmem(x):
    return pltpu.with_memory_space_constraint(x, pltpu.VMEM)


def in_hbm(x):
    return pltpu.with_memory_space_constraint(x, pltpu.HBM)


class Chain:
    def __init__(self, scalars):
        self.scalars, self.token = scalars, None


def call(body, name, chain, operands, in_specs, out_shape, out_specs, grid, aliases=None, copies=(), cost=0, vmem=VMEM):
    n_in, n_out, n = len(operands), len(out_shape), len(copies)
    aliases = dict(aliases or {})
    operands, in_specs = list(operands), list(in_specs)
    out_shape, out_specs = list(out_shape), list(out_specs)
    unread = []
    for k, (array, in_spec, space, shape, out_spec, into) in enumerate(copies):
        operands.append(array)
        in_specs.append(in_spec)
        out_shape.append(space(shape, array.dtype))
        out_specs.append(out_spec)
        if into is not None:
            aliases[1 + n_in + n + len(unread)] = n_out + k
            unread.append(into)
    if chain.token is not None:
        unread.append(chain.token)
    operands += unread
    out_shape.append(jax.ShapeDtypeStruct((8, 128), F32))

    def kernel(s, *refs):
        outs = refs[len(operands) :]
        body(s, *refs[:n_in], *outs[:n_out])
        for source, target in zip(refs[n_in : n_in + n], outs[n_out:]):
            target[...] = source[...].reshape(target.shape)

    *results, chain.token = pl.pallas_call(
        kernel,
        out_shape=out_shape,
        grid_spec=pltpu.PrefetchScalarGridSpec(
            num_scalar_prefetch=1,
            grid=grid,
            in_specs=in_specs + [ANY] * len(unread),
            out_specs=out_specs + [ANY],
        ),
        input_output_aliases=aliases,
        compiler_params=pltpu.CompilerParams(vmem_limit_bytes=vmem),
        cost_estimate=pl.CostEstimate(flops=cost, bytes_accessed=0, transcendentals=0),
        name=name,
    )(chain.scalars, *operands)
    return results


class Fsdp:
    def __init__(self, hidden_states, cotangent, weight, chain):
        self.states, self.cotans = in_hbm(hidden_states), in_hbm(cotangent)
        self.tokens, self.model = hidden_states.shape
        self.keys = cotangent.shape[1]
        self.devices = lax.axis_size("fsdp")
        self.rows = self.model // self.devices
        self.chain = chain
        self.whole = pl.BlockSpec((self.tokens, self.keys), lambda i, s: (0, 0), pipeline_mode=pl.Buffered(1))
        self.weight = in_hbm(lax.all_gather(weight, "fsdp", axis=0, tiled=True))
        self.sums = None

    def project(self, part, parts):
        block, depth = self.tokens // PROJECT_BLOCKS, self.model // parts
        first, final = part == 0, part == parts - 1
        rows = pl.BlockSpec((block, self.keys), lambda i, s: (i, 0))
        operands = [self.states, self.weight]
        in_specs = [
            pl.BlockSpec((block, depth), lambda i, s: (i, part)),
            pl.BlockSpec((depth, self.keys), lambda i, s: (part, 0), pipeline_mode=pl.Buffered(1)),
        ]
        aliases = {}
        if not first:
            operands.append(self.total)
            in_specs.append(rows)
            aliases = {} if final else {3: 0}

        def body(s, states, weight, *refs):
            total = jnp.dot(states[...], weight[...], preferred_element_type=F32)
            if not first:
                total = total + refs[0][...]
            refs[-1][...] = total.astype(refs[-1].dtype)

        (self.total,) = call(
            body, f"project_{part}", self.chain, operands, in_specs,
            [pltpu.HBM((self.tokens, self.keys), BF16) if final else pltpu.VMEM((self.tokens, self.keys), F32)], [rows],
            (PROJECT_BLOCKS,), aliases, vmem=VMEM_P,
        )

    def grad(self, first, n, copies=()):
        def body(s, states, cotans, *refs):
            refs[-1][0] = lax.dot_general(
                states[...], cotans[...], CONTRACT_ROWS, preferred_element_type=F32
            ).astype(BF16)

        operands = [self.states, self.cotans]
        in_specs = [pl.BlockSpec((self.tokens, self.rows), lambda i, s: (0, first + i)), self.whole]
        aliases = {}
        if self.sums is not None:
            operands.append(self.sums)
            in_specs.append(ANY)
            aliases = {3: 0}
        self.sums, *copied = call(
            body, f"grad_{first}", self.chain, operands, in_specs,
            [pltpu.HBM((self.devices, self.rows, self.keys), BF16)],
            [pl.BlockSpec((1, self.rows, self.keys), lambda i, s: (first + i, 0, 0))],
            (n,), aliases, copies=copies,
        )
        return copied

    def scatter(self):
        self.sums = lax.psum_scatter(
            self.sums.reshape(self.model, self.keys), "fsdp", scatter_dimension=0, tiled=True
        )

    def widen(self):
        def body(s, x, out):
            out[...] = x[...].astype(F32)

        each = pl.BlockSpec((self.rows // 2, self.keys), lambda i, s: (i, 0))
        (out,) = call(
            body, "widen", self.chain, [in_hbm(self.sums)], [each], [pltpu.HBM((self.rows, self.keys), F32)], [each], (2,)
        )
        return out


def own_term(g, m, replicas):
    return (GLOBAL_PART * g + MOMENT_PART * m) * (replicas / MEAN_PART)


def by_replica(replicas, s, body):
    for z in range(replicas):
        pl.when(s[REPLICA] == z)(functools.partial(body, z))


def way(z, side):
    return (z - 1 + side) % 2


def hops_of(z, replicas):
    return z - 1, replicas - 2 - z


def first_body(replicas, s, l, g, m, out):
    width = g.shape[2]

    def body(z):
        if 0 < z < replicas - 1:
            return
        columns = slice(z * width, (z + 1) * width)
        out[...] = l[0]
        out[:, columns] = (l[0, :, columns].astype(F32) + own_term(g[0], m[0], replicas)).astype(BF16)

    by_replica(replicas, s, body)


def round_body(replicas, old_of, ways, outs, keep, s, *refs):
    refs = list(refs)
    take = lambda n: [refs.pop(0) for _ in range(n)]
    came = take(2)
    old = dict(zip(old_of, take(len(old_of))))
    sources = take(3), take(3)
    width = sources[0][1].shape[2]
    kept = take(3) if outs else ()
    targets = take(ways)
    results = take(3) if outs else ()

    def body(z):
        columns = slice(z * width, (z + 1) * width)
        hops = hops_of(z, replicas)
        for side in (0, 1):
            target = way(z, 1 - side)
            if hops[1 - side] < 0 or target >= ways:
                continue
            l, g, m = sources[side]
            out = targets[target]
            if hops[side] < 0:
                out[...] = l[0]
                mine = l[0, :, columns].astype(F32)
            else:
                total = came[way(z, side)][...].astype(F32) + l[0].astype(F32)
                out[...] = total.astype(BF16)
                mine = total[:, columns]
            out[:, columns] = (mine + own_term(g[0], m[0], replicas)).astype(BF16)
        if not outs:
            return
        reach = max(hops)
        if reach in keep:
            for ref, before in zip(results, kept):
                ref[...] = before[...]
            return
        l, g, m = sources[0 if hops[0] == reach else 1]
        total = l[0].astype(F32)
        for side in (0, 1):
            if hops[side] >= 0:
                path = way(z, side)
                total = total + old.get((path, reach - hops[side]), came[path])[...].astype(F32)
        synced, new_g, new_m = results
        synced[...] = (total * (MEAN_PART / replicas)).astype(BF16)
        mean = total[:, columns] / replicas
        pseudo = g[0] - mean
        moment = 0.9 * m[0] + pseudo
        after = g[0] - 0.7 * (pseudo + 0.9 * moment)
        synced[:, columns] = after.astype(BF16)
        new_g[0] = after
        new_m[0] = moment

    by_replica(replicas, s, body)


class Line:
    def __init__(self, local_fragments, global_fragments, momentum, chain):
        self.replicas = lax.axis_size("replica")
        frags, layers, rows, keys = local_fragments.shape
        self.given = global_fragments.shape
        self.layers, self.rows, self.keys = layers, rows, keys
        self.width = global_fragments.shape[3]
        self.total = layers * rows
        unit = 16 * STEPS
        self.chunk = -(-self.total // (unit * PIECES)) * unit
        self.block = self.chunk // STEPS
        self.pieces = -(-self.total // self.chunk)
        self.local = in_hbm(local_fragments.reshape(frags, self.total, keys))
        self.outer = in_hbm(global_fragments.reshape(frags, self.total, self.width))
        self.moment = in_hbm(momentum.reshape(frags, self.total, self.width))
        self.last = self.pieces - 1 + DELAY * (self.replicas - 2)
        self.chain = chain
        self.sources, self.staged = [self.local, self.outer, self.moment], False
        self.staged_sources = [None] * 3
        self.piece = pl.BlockSpec((self.block, keys), lambda i, s: (i, 0))
        self.piece_shape = pltpu.VMEM((self.chunk, keys), BF16)
        self.state = None
        self.ready, self.came = [], []

    def pairs(self, t, path):
        n = self.replicas
        return [
            pair
            for z in range(n - 1)
            if z % 2 == path
            for pair, hop in (((z, z + 1), z), ((z + 1, z), n - 2 - z))
            if 0 <= t - DELAY * hop < self.pieces
        ]

    def ways(self, t):
        if t > self.last:
            return 0
        return 2 if self.pairs(t, 1) else 1

    def row(self, place, i):
        start = jnp.minimum(jnp.clip(place, 0, self.pieces - 1) * self.chunk, self.total - self.chunk)
        return pl.multiple_of(start + i * self.block, 16)

    def at(self, width, place, frag=lambda s: s[CHOSEN]):
        size = (pl.Element(1), pl.Element(self.block), pl.Element(width))
        return pl.BlockSpec(size, lambda i, s: (frag(s), self.row(place(s[REPLICA]), i), 0))

    def first(self, t):
        specs = [self.at(n, lambda z: t) for n in (self.keys, self.width, self.width)]
        self.ready.append(
            call(
                functools.partial(first_body, self.replicas), "first_sends", self.chain,
                [self.local, self.outer, self.moment], specs, [self.piece_shape], [self.piece], (STEPS,),
            )
        )

    def stage(self, k, steps):
        array = self.sources[k]
        steps = 2 ** (steps.bit_length() - 1)
        last = steps - 1
        size = (1, array.shape[1] // steps, array.shape[2])
        source = pl.BlockSpec(size, lambda i, s: (s[CHOSEN], jnp.minimum(i, last), 0))
        target = pl.BlockSpec(size, lambda i, s: (0, jnp.minimum(i, last), 0))
        return array, source, pltpu.VMEM, (1,) + array.shape[1:], target, None

    def idle(self, k, steps):
        array, state = (self.outer, self.moment)[k - 1], self.state[k]
        spec = pl.BlockSpec((1, array.shape[1] // steps, array.shape[2]), lambda i, s: (1 - s[CHOSEN], i, 0))
        return array, spec, pltpu.HBM, array.shape, spec, state

    def idle_all(self):
        copies = [self.idle(k, 4) for k in (1, 2)]
        self.state[1:] = call(lambda s: None, "idle", self.chain, [], [], [], [], (4,), copies=copies)

    def send(self, t):
        came = [lax.ppermute(x, "replica", self.pairs(t, path)) for path, x in enumerate(self.ready[t])]
        self.came.append((came + came)[:2])

    def round(self, t):
        n = self.replicas
        outs = t >= DELAY * min(max(hops_of(z, n)) for z in range(n))
        keep = {r for r in (max(hops_of(z, n)) for z in range(n)) if t > self.pieces - 1 + DELAY * r}
        users = {}
        for z in range(n):
            hops = hops_of(z, n)
            for side in (0, 1):
                behind = max(hops) - hops[side]
                if outs and hops[side] >= 0 and behind and t >= DELAY * behind:
                    users.setdefault((way(z, side), behind), []).append(z)
        old = [self.came[t - DELAY * behind][path] for path, behind in users]
        old_specs = [
            pl.BlockSpec(
                (self.block, self.keys),
                lambda i, s, zs=zs: (i * sum((s[REPLICA] == z).astype(jnp.int32) for z in zs), 0),
            )
            for zs in users.values()
        ]
        to_right = lambda z: t + DELAY - DELAY * z
        to_left = lambda z: t + DELAY - DELAY * (n - 1 - z)
        frag = (lambda s: 0) if self.staged else (lambda s: s[CHOSEN])
        specs = [self.at(w, place, frag) for place in (to_right, to_left) for w in (self.keys, self.width, self.width)]
        in_specs = [self.piece, self.piece] + old_specs + specs
        operands = list(self.came[t]) + old + self.sources * 2
        ways = self.ways(t + DELAY)
        out_shape, out_specs, aliases = [self.piece_shape] * ways, [self.piece] * ways, {}
        if outs:
            place = lambda z: t - DELAY * jnp.maximum(z - 1, n - 2 - z)
            flat = pl.BlockSpec(
                (pl.Element(self.block), pl.Element(self.keys)), lambda i, s: (self.row(place(s[REPLICA]), i), 0)
            )
            state_specs = [flat] + [self.at(self.width, place)] * 2
            if self.state is None:
                operands += [self.came[t][0]] * 3
                in_specs += [ANY] * 3
            else:
                aliases = {1 + len(operands) + k: ways + k for k in range(3)}
                operands += self.state
                in_specs += state_specs if keep else [ANY] * 3
            out_shape += [
                pltpu.HBM((self.total, self.keys), BF16),
                pltpu.HBM(self.outer.shape, F32),
                pltpu.HBM(self.moment.shape, F32),
            ]
            out_specs += state_specs
        if not out_shape:
            return
        results = call(
            functools.partial(round_body, n, list(users), ways, outs, keep), f"round_{t}", self.chain, operands, in_specs,
            out_shape, out_specs, (STEPS,), aliases, cost=LONG if t == self.last else 0, vmem=VMEM_R,
        )
        self.ready.append(results[:ways])
        if outs:
            self.state = list(results[ways:])

    def result(self):
        synced, new_global, new_momentum = self.state
        return (
            synced.reshape(self.layers, self.rows, self.keys),
            new_global.reshape(self.given),
            new_momentum.reshape(self.given),
        )


def shards(
    hidden_states,
    cotangent,
    key_weight,
    local_fragments,
    global_fragments,
    momentum,
    fragment_index,
):
    chosen = fragment_index[0] % FRAGS
    place = [lax.axis_index("replica"), lax.axis_index("fsdp")]
    chain = Chain(jnp.stack([chosen] + place).astype(jnp.int32))
    line = Line(local_fragments[0], global_fragments, momentum, chain)
    fsdp = Fsdp(hidden_states, cotangent, key_weight[0], chain)
    eighth = fsdp.devices // 8

    def grad(first, n, stage):
        steps = n * eighth
        copied = fsdp.grad(first * eighth, steps, [line.stage(k, steps) for k in stage])
        for k, array in zip(stage, copied):
            line.staged_sources[k] = array

    def work(t):
        for first, n, stage, then in GRADS:
            if t == then:
                grad(first, n, stage)
                if None not in line.staged_sources and not line.staged:
                    line.sources, line.staged = [in_vmem(x) for x in line.staged_sources], True
                if first + n == 8:
                    fsdp.scatter()
        if t in PROJECT_ROUNDS:
            fsdp.project(PROJECT_ROUNDS.index(t), len(PROJECT_ROUNDS))
        if t == line.last - IDLE_BEFORE:
            line.idle_all()

    for t in range(DELAY):
        line.first(t)
    work(-1)
    for t in range(line.last + 1):
        line.send(t)
        line.round(t)
        work(t)
    synced, new_global, new_momentum = line.result()
    weight_grad = fsdp.widen()
    return (fsdp.total, weight_grad[None], new_global, new_momentum, synced)


def solution(mesh):
    placed = (
        P(("replica", "fsdp"), None),
        P(("replica", "fsdp"), None),
        P("replica", "fsdp", None),
        P("replica", None, None, "fsdp", None),
        P(None, None, "fsdp", "replica"),
        P(None, None, "fsdp", "replica"),
        P(),
    )
    return jax.shard_map(
        shards,
        mesh=mesh,
        in_specs=placed,
        out_specs=(
            P(("replica", "fsdp"), None),
            P("replica", "fsdp", None),
            P(None, None, "fsdp", "replica"),
            P(None, None, "fsdp", "replica"),
            P(None, "fsdp", None),
        ),
        check_vma=False,
    )
```

```python
import functools

import jax
import jax.numpy as jnp
from jax import lax
from jax.experimental import pallas as pl
from jax.experimental.pallas import tpu as pltpu
from jax.sharding import PartitionSpec as P

FRAGS = 2
PIECES = 10
STEPS = 1
DELAY = 2
PROJECT_BLOCKS = 2
GRADS = ((0, 2, (0,), -1), (2, 3, (1, 2), 0), (5, 3, (), 2))
IDLE_BEFORE = 5
PROJECT_ROUNDS = (6, 10)
MEAN_PART = 1.33
GLOBAL_PART = -0.33
MOMENT_PART = -0.567
F32 = jnp.float32
BF16 = jnp.bfloat16
ANY = pl.BlockSpec(memory_space=pl.ANY)
CONTRACT_ROWS = (((0,), (0,)), ((), ()))
CHOSEN, REPLICA, FSDP = 0, 1, 2
VMEM = 14 << 20
VMEM_R = 10 << 20
VMEM_P = 24 << 20
LONG = 116 * 10**9


def in_vmem(x):
    return pltpu.with_memory_space_constraint(x, pltpu.VMEM)


def in_hbm(x):
    return pltpu.with_memory_space_constraint(x, pltpu.HBM)


class Chain:
    def __init__(self, scalars):
        self.scalars, self.token = scalars, None


def call(body, name, chain, operands, in_specs, out_shape, out_specs, grid, aliases=None, copies=(), cost=0, vmem=VMEM):
    n_in, n_out, n = len(operands), len(out_shape), len(copies)
    aliases = dict(aliases or {})
    operands, in_specs = list(operands), list(in_specs)
    out_shape, out_specs = list(out_shape), list(out_specs)
    unread = []
    for k, (array, in_spec, space, shape, out_spec, into) in enumerate(copies):
        operands.append(array)
        in_specs.append(in_spec)
        out_shape.append(space(shape, array.dtype))
        out_specs.append(out_spec)
        if into is not None:
            aliases[1 + n_in + n + len(unread)] = n_out + k
            unread.append(into)
    if chain.token is not None:
        unread.append(chain.token)
    operands += unread
    out_shape.append(jax.ShapeDtypeStruct((8, 128), F32))

    def kernel(s, *refs):
        outs = refs[len(operands) :]
        body(s, *refs[:n_in], *outs[:n_out])
        for source, target in zip(refs[n_in : n_in + n], outs[n_out:]):
            target[...] = source[...].reshape(target.shape)

    *results, chain.token = pl.pallas_call(
        kernel,
        out_shape=out_shape,
        grid_spec=pltpu.PrefetchScalarGridSpec(
            num_scalar_prefetch=1,
            grid=grid,
            in_specs=in_specs + [ANY] * len(unread),
            out_specs=out_specs + [ANY],
        ),
        input_output_aliases=aliases,
        compiler_params=pltpu.CompilerParams(vmem_limit_bytes=vmem),
        cost_estimate=pl.CostEstimate(flops=cost, bytes_accessed=0, transcendentals=0),
        name=name,
    )(chain.scalars, *operands)
    return results


class Fsdp:
    def __init__(self, hidden_states, cotangent, weight, chain):
        self.states, self.cotans = in_hbm(hidden_states), in_hbm(cotangent)
        self.tokens, self.model = hidden_states.shape
        self.keys = cotangent.shape[1]
        self.devices = lax.axis_size("fsdp")
        self.rows = self.model // self.devices
        self.chain = chain
        self.whole = pl.BlockSpec((self.tokens, self.keys), lambda i, s: (0, 0), pipeline_mode=pl.Buffered(1))
        self.weight = in_hbm(lax.all_gather(weight, "fsdp", axis=0, tiled=True))
        self.sums = None

    def project(self, part, parts):
        block, depth = self.tokens // PROJECT_BLOCKS, self.model // parts
        first, final = part == 0, part == parts - 1
        rows = pl.BlockSpec((block, self.keys), lambda i, s: (i, 0))
        operands = [self.states, self.weight]
        in_specs = [
            pl.BlockSpec((block, depth), lambda i, s: (i, part)),
            pl.BlockSpec((depth, self.keys), lambda i, s: (part, 0), pipeline_mode=pl.Buffered(1)),
        ]
        aliases = {}
        if not first:
            operands.append(self.total)
            in_specs.append(rows)
            aliases = {} if final else {3: 0}

        def body(s, states, weight, *refs):
            total = jnp.dot(states[...], weight[...], preferred_element_type=F32)
            if not first:
                total = total + refs[0][...]
            refs[-1][...] = total.astype(refs[-1].dtype)

        (self.total,) = call(
            body, f"project_{part}", self.chain, operands, in_specs,
            [pltpu.HBM((self.tokens, self.keys), BF16) if final else pltpu.VMEM((self.tokens, self.keys), F32)], [rows],
            (PROJECT_BLOCKS,), aliases, vmem=VMEM_P,
        )

    def grad(self, first, n, copies=()):
        def body(s, states, cotans, *refs):
            refs[-1][0] = lax.dot_general(
                states[...], cotans[...], CONTRACT_ROWS, preferred_element_type=F32
            ).astype(BF16)

        operands = [self.states, self.cotans]
        in_specs = [pl.BlockSpec((self.tokens, self.rows), lambda i, s: (0, first + i)), self.whole]
        aliases = {}
        if self.sums is not None:
            operands.append(self.sums)
            in_specs.append(ANY)
            aliases = {3: 0}
        self.sums, *copied = call(
            body, f"grad_{first}", self.chain, operands, in_specs,
            [pltpu.HBM((self.devices, self.rows, self.keys), BF16)],
            [pl.BlockSpec((1, self.rows, self.keys), lambda i, s: (first + i, 0, 0))],
            (n,), aliases, copies=copies,
        )
        return copied

    def scatter(self):
        self.sums = lax.psum_scatter(
            self.sums.reshape(self.model, self.keys), "fsdp", scatter_dimension=0, tiled=True
        )

    def widen(self):
        def body(s, x, out):
            out[...] = x[...].astype(F32)

        each = pl.BlockSpec((self.rows // 2, self.keys), lambda i, s: (i, 0))
        (out,) = call(
            body, "widen", self.chain, [in_hbm(self.sums)], [each], [pltpu.HBM((self.rows, self.keys), F32)], [each], (2,)
        )
        return out


def own_term(g, m, replicas):
    return (GLOBAL_PART * g + MOMENT_PART * m) * (replicas / MEAN_PART)


def by_replica(replicas, s, body):
    for z in range(replicas):
        pl.when(s[REPLICA] == z)(functools.partial(body, z))


def way(z, side):
    return (z - 1 + side) % 2


def hops_of(z, replicas):
    return z - 1, replicas - 2 - z


def first_body(replicas, s, l, g, m, out):
    width = g.shape[2]

    def body(z):
        if 0 < z < replicas - 1:
            return
        columns = slice(z * width, (z + 1) * width)
        out[...] = l[0]
        out[:, columns] = (l[0, :, columns].astype(F32) + own_term(g[0], m[0], replicas)).astype(BF16)

    by_replica(replicas, s, body)


def round_body(replicas, old_of, ways, outs, keep, s, *refs):
    refs = list(refs)
    take = lambda n: [refs.pop(0) for _ in range(n)]
    came = take(2)
    old = dict(zip(old_of, take(len(old_of))))
    sources = take(3), take(3)
    width = sources[0][1].shape[2]
    kept = take(3) if outs else ()
    targets = take(ways)
    results = take(3) if outs else ()

    def body(z):
        columns = slice(z * width, (z + 1) * width)
        hops = hops_of(z, replicas)
        for side in (0, 1):
            target = way(z, 1 - side)
            if hops[1 - side] < 0 or target >= ways:
                continue
            l, g, m = sources[side]
            out = targets[target]
            if hops[side] < 0:
                out[...] = l[0]
                mine = l[0, :, columns].astype(F32)
            else:
                total = came[way(z, side)][...].astype(F32) + l[0].astype(F32)
                out[...] = total.astype(BF16)
                mine = total[:, columns]
            out[:, columns] = (mine + own_term(g[0], m[0], replicas)).astype(BF16)
        if not outs:
            return
        reach = max(hops)
        if reach in keep:
            for ref, before in zip(results, kept):
                ref[...] = before[...]
            return
        l, g, m = sources[0 if hops[0] == reach else 1]
        total = l[0].astype(F32)
        for side in (0, 1):
            if hops[side] >= 0:
                path = way(z, side)
                total = total + old.get((path, reach - hops[side]), came[path])[...].astype(F32)
        synced, new_g, new_m = results
        synced[...] = (total * (MEAN_PART / replicas)).astype(BF16)
        mean = total[:, columns] / replicas
        pseudo = g[0] - mean
        moment = 0.9 * m[0] + pseudo
        after = g[0] - 0.7 * (pseudo + 0.9 * moment)
        synced[:, columns] = after.astype(BF16)
        new_g[0] = after
        new_m[0] = moment

    by_replica(replicas, s, body)


class Line:
    def __init__(self, local_fragments, global_fragments, momentum, chain):
        self.replicas = lax.axis_size("replica")
        frags, layers, rows, keys = local_fragments.shape
        self.given = global_fragments.shape
        self.layers, self.rows, self.keys = layers, rows, keys
        self.width = global_fragments.shape[3]
        self.total = layers * rows
        unit = 16 * STEPS
        self.chunk = -(-self.total // (unit * PIECES)) * unit
        self.block = self.chunk // STEPS
        self.pieces = -(-self.total // self.chunk)
        self.local = in_hbm(local_fragments.reshape(frags, self.total, keys))
        self.outer = in_hbm(global_fragments.reshape(frags, self.total, self.width))
        self.moment = in_hbm(momentum.reshape(frags, self.total, self.width))
        self.last = self.pieces - 1 + DELAY * (self.replicas - 2)
        self.chain = chain
        self.sources, self.staged = [self.local, self.outer, self.moment], False
        self.staged_sources = [None] * 3
        self.piece = pl.BlockSpec((self.block, keys), lambda i, s: (i, 0))
        self.piece_shape = pltpu.VMEM((self.chunk, keys), BF16)
        self.state = None
        self.ready, self.came = [], []

    def pairs(self, t, path):
        n = self.replicas
        return [
            pair
            for z in range(n - 1)
            if z % 2 == path
            for pair, hop in (((z, z + 1), z), ((z + 1, z), n - 2 - z))
            if 0 <= t - DELAY * hop < self.pieces
        ]

    def ways(self, t):
        if t > self.last:
            return 0
        return 2 if self.pairs(t, 1) else 1

    def row(self, place, i):
        start = jnp.minimum(jnp.clip(place, 0, self.pieces - 1) * self.chunk, self.total - self.chunk)
        return pl.multiple_of(start + i * self.block, 16)

    def at(self, width, place, frag=lambda s: s[CHOSEN]):
        size = (pl.Element(1), pl.Element(self.block), pl.Element(width))
        return pl.BlockSpec(size, lambda i, s: (frag(s), self.row(place(s[REPLICA]), i), 0))

    def first(self, t):
        specs = [self.at(n, lambda z: t) for n in (self.keys, self.width, self.width)]
        self.ready.append(
            call(
                functools.partial(first_body, self.replicas), "first_sends", self.chain,
                [self.local, self.outer, self.moment], specs, [self.piece_shape], [self.piece], (STEPS,),
            )
        )

    def stage(self, k, steps):
        array = self.sources[k]
        steps = 2 ** (steps.bit_length() - 1)
        last = steps - 1
        size = (1, array.shape[1] // steps, array.shape[2])
        source = pl.BlockSpec(size, lambda i, s: (s[CHOSEN], jnp.minimum(i, last), 0))
        target = pl.BlockSpec(size, lambda i, s: (0, jnp.minimum(i, last), 0))
        return array, source, pltpu.VMEM, (1,) + array.shape[1:], target, None

    def idle(self, k, steps):
        array, state = (self.outer, self.moment)[k - 1], self.state[k]
        spec = pl.BlockSpec((1, array.shape[1] // steps, array.shape[2]), lambda i, s: (1 - s[CHOSEN], i, 0))
        return array, spec, pltpu.HBM, array.shape, spec, state

    def idle_all(self):
        copies = [self.idle(k, 4) for k in (1, 2)]
        self.state[1:] = call(lambda s: None, "idle", self.chain, [], [], [], [], (4,), copies=copies)

    def send(self, t):
        came = [lax.ppermute(x, "replica", self.pairs(t, path)) for path, x in enumerate(self.ready[t])]
        self.came.append((came + came)[:2])

    def round(self, t):
        n = self.replicas
        outs = t >= DELAY * min(max(hops_of(z, n)) for z in range(n))
        keep = {r for r in (max(hops_of(z, n)) for z in range(n)) if t > self.pieces - 1 + DELAY * r}
        users = {}
        for z in range(n):
            hops = hops_of(z, n)
            for side in (0, 1):
                behind = max(hops) - hops[side]
                if outs and hops[side] >= 0 and behind and t >= DELAY * behind:
                    users.setdefault((way(z, side), behind), []).append(z)
        old = [self.came[t - DELAY * behind][path] for path, behind in users]
        old_specs = [
            pl.BlockSpec(
                (self.block, self.keys),
                lambda i, s, zs=zs: (i * sum((s[REPLICA] == z).astype(jnp.int32) for z in zs), 0),
            )
            for zs in users.values()
        ]
        to_right = lambda z: t + DELAY - DELAY * z
        to_left = lambda z: t + DELAY - DELAY * (n - 1 - z)
        frag = (lambda s: 0) if self.staged else (lambda s: s[CHOSEN])
        specs = [self.at(w, place, frag) for place in (to_right, to_left) for w in (self.keys, self.width, self.width)]
        in_specs = [self.piece, self.piece] + old_specs + specs
        operands = list(self.came[t]) + old + self.sources * 2
        ways = self.ways(t + DELAY)
        out_shape, out_specs, aliases = [self.piece_shape] * ways, [self.piece] * ways, {}
        if outs:
            place = lambda z: t - DELAY * jnp.maximum(z - 1, n - 2 - z)
            flat = pl.BlockSpec(
                (pl.Element(self.block), pl.Element(self.keys)), lambda i, s: (self.row(place(s[REPLICA]), i), 0)
            )
            state_specs = [flat] + [self.at(self.width, place)] * 2
            if self.state is None:
                operands += [self.came[t][0]] * 3
                in_specs += [ANY] * 3
            else:
                aliases = {1 + len(operands) + k: ways + k for k in range(3)}
                operands += self.state
                in_specs += state_specs if keep else [ANY] * 3
            out_shape += [
                pltpu.HBM((self.total, self.keys), BF16),
                pltpu.HBM(self.outer.shape, F32),
                pltpu.HBM(self.moment.shape, F32),
            ]
            out_specs += state_specs
        if not out_shape:
            return
        results = call(
            functools.partial(round_body, n, list(users), ways, outs, keep), f"round_{t}", self.chain, operands, in_specs,
            out_shape, out_specs, (STEPS,), aliases, cost=LONG if t == self.last else 0, vmem=VMEM_R,
        )
        self.ready.append(results[:ways])
        if outs:
            self.state = list(results[ways:])

    def result(self):
        synced, new_global, new_momentum = self.state
        return (
            synced.reshape(self.layers, self.rows, self.keys),
            new_global.reshape(self.given),
            new_momentum.reshape(self.given),
        )


def shards(
    hidden_states,
    cotangent,
    key_weight,
    local_fragments,
    global_fragments,
    momentum,
    fragment_index,
):
    chosen = fragment_index[0] % FRAGS
    place = [lax.axis_index("replica"), lax.axis_index("fsdp")]
    chain = Chain(jnp.stack([chosen] + place).astype(jnp.int32))
    line = Line(local_fragments[0], global_fragments, momentum, chain)
    fsdp = Fsdp(hidden_states, cotangent, key_weight[0], chain)
    eighth = fsdp.devices // 8

    def grad(first, n, stage):
        steps = n * eighth
        copied = fsdp.grad(first * eighth, steps, [line.stage(k, steps) for k in stage])
        for k, array in zip(stage, copied):
            line.staged_sources[k] = array

    def work(t):
        for first, n, stage, then in GRADS:
            if t == then:
                grad(first, n, stage)
                if None not in line.staged_sources and not line.staged:
                    line.sources, line.staged = [in_vmem(x) for x in line.staged_sources], True
                if first + n == 8:
                    fsdp.scatter()
        if t in PROJECT_ROUNDS:
            fsdp.project(PROJECT_ROUNDS.index(t), len(PROJECT_ROUNDS))
        if t == line.last - IDLE_BEFORE:
            line.idle_all()

    for t in range(DELAY):
        line.first(t)
    work(-1)
    for t in range(line.last + 1):
        line.send(t)
        line.round(t)
        work(t)
    synced, new_global, new_momentum = line.result()
    weight_grad = fsdp.widen()
    return (fsdp.total, weight_grad[None], new_global, new_momentum, synced)


def solution(mesh):
    placed = (
        P(("replica", "fsdp"), None),
        P(("replica", "fsdp"), None),
        P("replica", "fsdp", None),
        P("replica", None, None, "fsdp", None),
        P(None, None, "fsdp", "replica"),
        P(None, None, "fsdp", "replica"),
        P(),
    )
    return jax.shard_map(
        shards,
        mesh=mesh,
        in_specs=placed,
        out_specs=(
            P(("replica", "fsdp"), None),
            P("replica", "fsdp", None),
            P(None, None, "fsdp", "replica"),
            P(None, None, "fsdp", "replica"),
            P(None, "fsdp", None),
        ),
        check_vma=False,
    )
```
